512 devices in a mesh: tok: 16 (over x, z_hi, core), feat: 32 (over y, z_lo).
Axes of the slice: x: 4, y: 8, z: 8 (z_hi: 2, z_lo: 4; z = z_hi * 4 + z_lo), core: 2. Of those that a mesh axis runs over, the one named last changes fastest.
Arguments:
- tokens: bfloat16 [16384, 16384], P('tok', 'feat'), parts along dimension 0, may hold values from -6 to 6
- butterfly: bfloat16 [6, 512, 16384], P(None, None, 'feat'), may hold values from -0.109375 to 0.109375
- rank_down: bfloat16 [16384, 512], P('feat'), may hold values from -0.046875 to 0.046875
- rank_up: bfloat16 [512, 16384], P(None, 'feat'), may hold values from -0.25 to 0.25
Outputs:
- mixed: bfloat16 [16384, 16384], P('tok', 'feat'), parts along dimension 0
The draws below stay inside these ranges and needn't reach their ends.
There are 16 independent parts, one for each index of `tok`. The reference program is written for one: setup_inputs(seed, part) draws one part's arguments, and reference() takes and returns one part's arrays. A program takes and returns all parts, laid end to end along the dimension named above; an argument that names none is the same for every part. Nothing has to cross between parts.
All inputs are finite; a program needn't handle non-finite values.
Results may differ from the reference program's by a relative error of at most 0.004.
Values may be sent and summed in bfloat16 or wider, within the bound.
A program may use at most 64 MiB of HBM per device.

```python
import jax
import jax.numpy as jnp
import numpy as np

BLOCK = 512
RANK = 512
TOK = 1024
H = 16384
PARTNERS = 6
N_FEAT = 32


def levels(key, dims, pieces, low, largest):
    gain, own = 1.0, jax.random.fold_in(key, 6)
    for dim, shards_of in pieces:
        heights = jnp.exp(jax.random.uniform(jax.random.fold_in(own, dim), (shards_of,), jnp.float32, low / len(pieces), largest / len(pieces)))
        gain = gain * jnp.repeat(heights, dims[dim] // shards_of).reshape([-1 if axis == dim else 1 for axis in range(len(dims))])
    return gain


def bell_draw(own_key, dims, spread, bound, cuts=(), held_as=jnp.bfloat16):
    factor_of = levels(own_key, dims, cuts, -0.22, 0.18) if cuts else 1.0
    values = jax.random.normal(own_key, dims, jnp.float32) * spread * factor_of
    return jnp.minimum(jnp.maximum(values, -bound), bound).astype(held_as)


def setup_inputs(seed: int = 0, part: int = 0) -> dict:
    seeds = jax.random.split(jax.random.key(seed), 5)
    own_keys = jax.random.split(jax.random.fold_in(seeds[4], part), 5)
    return {
        "tokens": bell_draw(own_keys[0], (TOK, H), 1.0, 6.0, ((1, 32),)),
        "butterfly": bell_draw(seeds[1], (PARTNERS, BLOCK, H), (PARTNERS * BLOCK) ** -0.5, 0.109375, ((2, 32),)),
        "rank_down": bell_draw(seeds[2], (H, RANK), H ** -0.5, 0.046875, ((0, 32),)),
        "rank_up": bell_draw(seeds[3], (RANK, H), RANK ** -0.5, 0.25, ((1, 32),)),
    }


def reference(tokens, butterfly, rank_down, rank_up):
    count = tokens.shape[0]
    blocks = tokens.reshape(count, N_FEAT, BLOCK).astype(jnp.float32)
    sparse = jnp.zeros((count, N_FEAT, BLOCK), jnp.float32)
    for level in range(PARTNERS):
        if level == 0:
            partner_order = np.arange(N_FEAT)
        else:
            partner_order = np.arange(N_FEAT) ^ (1 << (level - 1))
        source = blocks[:, partner_order, :]
        weights = butterfly[level].reshape(BLOCK, N_FEAT, BLOCK).astype(jnp.float32)
        sparse = sparse + jnp.einsum("tnc,cnd->tnd", source, weights)
    rank_mid = jnp.dot(tokens, rank_down, preferred_element_type=jnp.float32).astype(jnp.bfloat16)
    dense = sparse.reshape(count, H) + jnp.dot(rank_mid, rank_up, preferred_element_type=jnp.float32)
    return jax.nn.gelu(dense, approximate=False).astype(jnp.bfloat16)
```

```python
import functools

import jax
import jax.numpy as jnp
from jax import lax
from jax.experimental import pallas as pl
from jax.experimental.pallas import tpu as pltpu
from jax.sharding import PartitionSpec as P

CHUNKS = 8
AHEAD = 2
STEPS_AT = {0: ["down1"], 1: ["down2"], 2: ["spread"], 3: ["gather"], 4: ["up0"], 5: ["up1"], 6: ["up2"], 7: ["up3"]}
Z_SENT = {0: 0, 1: 1, 2: 2, 3: 4, 4: 5, 5: 6, 6: 7, 7: 8}
NY, NZ = 8, 4
F32, BF16 = jnp.float32, jnp.bfloat16


def dot(a, b):
    return jnp.dot(a, b, preferred_element_type=F32)


def kernel(tok, bfly, down, up, out,
           x, w, wd, wu, got, acc, part, box, from_low, from_high, mine, shares, share_in, mid, o,
           load_sem, send_own, got_sem, pass_sem, down_send, low_sem, high_sem, spread_send, spread_recv,
           gather_send, gather_recv, up_send_r, up_send_l, up_recv, out_sem):
    rows = tok.shape[0]
    step = rows // CHUNKS
    quarter = rows // NZ
    piece = quarter // NY
    me = lax.axis_index("feat")
    y, z = me // NZ, me % NZ
    c = y % 4
    inner = (c == 1) | (c == 2)
    b0, b1, b2 = y % 2, (y // 2) % 2, y // 4
    y1 = y + 1 - 2 * b0
    y2 = y + 2 - 4 * b1
    y3 = y1 + 2 - 4 * b1
    y6 = y2 + 4 - 8 * b2
    z1 = z + 1 - 2 * (z % 2)
    z2 = z + 2 - 4 * (z // 2)

    def at(yy, zz):
        return {"feat": yy * NZ + zz}

    def remote(src, dst, ssem, rsem, yy, zz):
        return pltpu.make_async_remote_copy(
            src_ref=src, dst_ref=dst, send_sem=ssem, recv_sem=rsem,
            device_id=at(yy, zz), device_id_type=pl.DeviceIdType.MESH)

    loads = [
        pltpu.make_async_copy(tok, x, load_sem.at[0]),
        pltpu.make_async_copy(down, wd, load_sem.at[1]),
        pltpu.make_async_copy(bfly, w, load_sem.at[2]),
        pltpu.make_async_copy(up, wu, load_sem.at[3]),
    ]
    for load in loads:
        load.start()

    barrier = pltpu.get_barrier_semaphore()
    peers = [(lax.rem(y + d, NY), z) for d in range(1, NY)] + [(y, lax.rem(z + d, NZ)) for d in range(1, NZ)]
    for yy, zz in peers:
        pl.semaphore_signal(barrier, inc=1, device_id=at(yy, zz), device_id_type=pl.DeviceIdType.MESH)
    pl.semaphore_wait(barrier, len(peers))

    def chunk(k):
        return pl.ds(k * step, step)

    def own(slot, k, yy, zz):
        return remote(tok.at[chunk(k)], got.at[slot, chunk(k)], send_own.at[slot, k], got_sem.at[slot, k], yy, zz)

    def passed(src, slot, k, yy):
        return remote(got.at[src, chunk(k)], got.at[slot, chunk(k)], pass_sem.at[src, k], got_sem.at[slot, k], yy, z)

    def send_y(k):
        @pl.when(inner)
        def _():
            own(1, k, y2, z).start()
        own(0, k, y1, z).start()

    def send_z(k):
        own(3, k, y, z1).start()
        own(4, k, y, z2).start()

    def wait_got(slot, k):
        own(slot, k, y1, z).wait_recv()

    def share(j):
        return pl.ds(pl.multiple_of(j * quarter, quarter), quarter)

    def toward_high(j):
        return remote(box.at[share(j)], from_low.at[j], down_send.at[j], low_sem.at[j], y, z + 1)

    def toward_low(j):
        return remote(box.at[share(j)], from_high.at[j], down_send.at[j], high_sem.at[j], y, z - 1)

    def down_step(s):
        @pl.when(z <= s)
        def _():
            j = NZ - 1 - s + z

            @pl.when(z > 0)
            def _():
                toward_high(j).wait_recv()
                box[share(j), :] = (part[share(j), :] + from_low[j].astype(F32)).astype(BF16)

            @pl.when(z == 0)
            def _():
                box[share(j), :] = part[share(j), :].astype(BF16)
            toward_high(j).start()

        @pl.when(z >= NZ - 1 - s)
        def _():
            j = s - (NZ - 1) + z

            @pl.when(z < NZ - 1)
            def _():
                toward_low(j).wait_recv()
                box[share(j), :] = (part[share(j), :] + from_high[j].astype(F32)).astype(BF16)

            @pl.when(z == NZ - 1)
            def _():
                box[share(j), :] = part[share(j), :].astype(BF16)
            toward_low(j).start()

    def piece_at(yy):
        return pl.ds(pl.multiple_of(yy * piece, piece), piece)

    def spread_copy(d):
        yy = lax.rem(y + d, NY)
        return remote(shares.at[piece_at(yy)], share_in.at[d - 1], spread_send.at[d - 1], spread_recv.at[d - 1], yy, z)

    def spread():
        mine[...] = part[share(z), :]

        @pl.when(z > 0)
        def _():
            toward_high(z).wait_recv()
            mine[...] += from_low[z].astype(F32)

        @pl.when(z < NZ - 1)
        def _():
            toward_low(z).wait_recv()
            mine[...] += from_high[z].astype(F32)
        shares[...] = mine[...].astype(BF16)
        for d in (4, 3, 5, 2, 6, 1, 7):
            spread_copy(d).start()

    def mid_piece(yy):
        return mid.at[pl.ds(pl.multiple_of(z * quarter + yy * piece, piece), piece)]

    def gather_copy(d):
        return remote(mid_piece(y), mid_piece(y), gather_send.at[d - 1], gather_recv.at[d - 1], lax.rem(y + d, NY), z)

    def gather():
        total = mine[piece_at(y), :]
        for d in range(1, NY):
            spread_copy(d).wait_recv()
            total += share_in[d - 1].astype(F32)
        mid[pl.ds(pl.multiple_of(z * quarter + y * piece, piece), piece), :] = total.astype(BF16)
        for d in (4, 3, 5, 2, 6, 1, 7):
            gather_copy(d).start()

    def up_right(j, s):
        return remote(mid.at[share(j)], mid.at[share(j)], up_send_r.at[s], up_recv.at[j], y, z + 1)

    def up_left(j, s):
        return remote(mid.at[share(j)], mid.at[share(j)], up_send_l.at[s], up_recv.at[j], y, z - 1)

    def up_step(s):
        if s == 0:
            for d in range(1, NY):
                gather_copy(d).wait_recv()
        low, high = z - s, z + s

        @pl.when(low >= 0)
        def _():
            if s:
                up_right(low, 0).wait_recv()
            if s < NZ - 1:
                @pl.when(z < NZ - 1)
                def _():
                    up_right(low, s).start()

        @pl.when(high < NZ)
        def _():
            if s:
                up_left(high, 0).wait_recv()
            if s < NZ - 1:
                @pl.when(z > 0)
                def _():
                    up_left(high, s).start()

    steps = {
        "down1": lambda: down_step(1), "down2": lambda: down_step(2), "spread": spread, "gather": gather,
        "up0": lambda: up_step(0), "up1": lambda: up_step(1), "up2": lambda: up_step(2), "up3": lambda: up_step(3),
    }

    for k in range(AHEAD):
        send_y(k)

    loads[0].wait()
    loads[1].wait()

    @pl.loop(0, NZ)
    def _(j):
        part[share(j), :] = dot(x[share(j), :], wd[...])
    down_step(0)
    loads[2].wait()
    loads[3].wait()

    def turn_b(k):
        wait_got(1, k)
        passed(1, 2, k, y6).start()
        acc[chunk(k), :] = dot(x[chunk(k), :], w[0]) + dot(got[0, chunk(k), :], w[3]) + dot(got[1, chunk(k), :], w[4])

    z_sent = 0
    for t in range(CHUNKS):
        if t + AHEAD < CHUNKS:
            send_y(t + AHEAD)
        wait_got(0, t)

        @pl.when(inner)
        def _():
            passed(0, 1, t, y3).start()
        for name in STEPS_AT.get(t, ()):
            steps[name]()
        for k in range(z_sent, Z_SENT[t]):
            send_z(k)
        z_sent = Z_SENT[t]
        if t:
            turn_b(t - 1)
    turn_b(CHUNKS - 1)

    outs = []
    for k in range(CHUNKS):
        wait_got(3, k)
        wait_got(4, k)
        wait_got(2, k)
        rows_k = chunk(k)
        dense = (acc[rows_k, :] + dot(got[3, rows_k, :], w[1]) + dot(got[4, rows_k, :], w[2])
                 + dot(got[2, rows_k, :], w[5]) + dot(mid[rows_k, :], wu[...]))
        o[rows_k, :] = (0.5 * dense * (1.0 + lax.erf(dense * 0.7071067811865476))).astype(BF16)
        store = pltpu.make_async_copy(o.at[rows_k], out.at[rows_k], out_sem.at[k])
        store.start()
        outs.append(store)

    for k in range(CHUNKS):
        own(0, k, y1, z).wait_send()
        own(3, k, y, z1).wait_send()
        own(4, k, y, z2).wait_send()
        passed(1, 2, k, y6).wait_send()

        @pl.when(inner)
        def _():
            own(1, k, y2, z).wait_send()
            passed(0, 1, k, y3).wait_send()
    for d in range(1, NY):
        spread_copy(d).wait_send()
        gather_copy(d).wait_send()
    for j in range(NZ):
        @pl.when(z != j)
        def _():
            toward_high(j).wait_send()
    for s in range(NZ - 1):
        @pl.when((z - s >= 0) & (z < NZ - 1))
        def _():
            up_right(z, s).wait_send()

        @pl.when((z + s < NZ) & (z > 0))
        def _():
            up_left(z, s).wait_send()
    for store in outs:
        store.wait()


def shards(tokens, butterfly, rank_down, rank_up):
    rows, width = tokens.shape
    rank = rank_down.shape[1]
    quarter = rows // NZ
    piece = quarter // NY
    dma = pltpu.SemaphoreType.DMA
    vmem = pltpu.VMEM
    anywhere = pl.BlockSpec(memory_space=pl.ANY)
    return pl.pallas_call(
        kernel,
        out_shape=jax.ShapeDtypeStruct((rows, width), BF16),
        in_specs=[anywhere] * 4,
        out_specs=anywhere,
        scratch_shapes=[
            vmem((rows, width), BF16),
            vmem(butterfly.shape, BF16),
            vmem(rank_down.shape, BF16),
            vmem(rank_up.shape, BF16),
            vmem((5, rows, width), BF16),
            vmem((rows, width), F32),
            vmem((rows, rank), F32),
            vmem((rows, rank), BF16),
            vmem((NZ, quarter, rank), BF16),
            vmem((NZ, quarter, rank), BF16),
            vmem((quarter, rank), F32),
            vmem((quarter, rank), BF16),
            vmem((NY - 1, piece, rank), BF16),
            vmem((rows, rank), BF16),
            vmem((rows, width), BF16),
            dma((4,)), dma((5, CHUNKS)), dma((5, CHUNKS)), dma((2, CHUNKS)),
            dma((NZ,)), dma((NZ,)), dma((NZ,)), dma((NY - 1,)), dma((NY - 1,)),
            dma((NY - 1,)), dma((NY - 1,)), dma((NZ - 1,)), dma((NZ - 1,)), dma((NZ,)), dma((CHUNKS,)),
        ],
        compiler_params=pltpu.CompilerParams(
            collective_id=0, has_side_effects=True, vmem_limit_bytes=48 * 2**20),
        cost_estimate=pl.CostEstimate(
            flops=2 * rows * width * width * 8, bytes_accessed=6 * 2**20, transcendentals=rows * width),
    )(tokens, butterfly, rank_down, rank_up)


def solution(mesh):
    return jax.shard_map(
        shards,
        mesh=mesh,
        in_specs=(P("tok", "feat"), P(None, None, "feat"), P("feat", None), P(None, "feat")),
        out_specs=P("tok", "feat"),
        check_vma=False,
    )
```

```python
import functools

import jax
import jax.numpy as jnp
from jax import lax
from jax.experimental import pallas as pl
from jax.experimental.pallas import tpu as pltpu
from jax.sharding import PartitionSpec as P

CHUNKS = 8
GROUPS = 2


def plan():
    order = [('y', 0), ('m', 0), ('d', 0), ('d', 1), ('w', 0), ('y', 1), ('a', 0), ('d', 2), ('d', 3), ('z', 0), ('y', 2), ('a', 1), ('b', 0), ('d', 4), ('d', 5), ('z', 1), ('z', 2), ('p', 0), ('y', 3), ('a', 2), ('b', 1), ('h', 0), ('h', 1), ('z', 3), ('z', 4), ('p', 1), ('y', 4), ('a', 3), ('b', 2), ('s', 0), ('s', 1), ('g', 0), ('g', 1), ('z', 5), ('z', 6), ('p', 2), ('y', 5), ('a', 4), ('b', 3), ('j', 0), ('j', 1), ('z', 7), ('p', 3), ('y', 6), ('a', 5), ('b', 4), ('u', 0), ('u', 1), ('p', 4), ('y', 7), ('a', 6), ('b', 5), ('u', 2), ('u', 3), ('p', 5), ('a', 7), ('b', 6), ('u', 4), ('u', 5), ('p', 6), ('b', 7), ('u', 6), ('u', 7), ('p', 7), ('f', 0), ('f', 1), ('f', 2), ('f', 3), ('f', 4), ('f', 5), ('f', 6), ('f', 7)]
    return order


NY, NZ = 8, 4
F32, BF16 = jnp.float32, jnp.bfloat16


def dot(a, b):
    return jnp.dot(a, b, preferred_element_type=F32)


def kernel(tok, bfly, down, up, out,
           x, w, wd, wu, got, acc, part, box, from_low, from_high, mine, shares, pair_in, share_in, mid, o,
           load_sem, send_own, got_sem, pass_sem, down_send, low_sem, high_sem, halve_send, halve_recv, spread_send, spread_recv,
           gather_send, gather_recv, join_send, join_recv, up_send_r, up_send_l, up_recv, out_sem):
    rows = tok.shape[0]
    step = rows // CHUNKS
    quarter = rows // NZ
    part_rows = quarter // GROUPS
    half = part_rows // 2
    piece = part_rows // NY
    me = lax.axis_index("feat")
    y, z = me // NZ, me % NZ
    b0, b1, b2 = y % 2, (y // 2) % 2, y // 4
    y1 = y + 1 - 2 * b0
    y2 = y + 2 - 4 * b1
    y6 = y2 + 4 - 8 * b2
    mate = lax.rem(y + NY - 1 + 2 * b0, NY)
    z1 = z + 1 - 2 * (z % 2)
    z2 = z + 2 - 4 * (z // 2)

    def at(yy, zz):
        return {"feat": yy * NZ + zz}

    def remote(src, dst, ssem, rsem, yy, zz):
        return pltpu.make_async_remote_copy(
            src_ref=src, dst_ref=dst, send_sem=ssem, recv_sem=rsem,
            device_id=at(yy, zz), device_id_type=pl.DeviceIdType.MESH)

    loads = [
        pltpu.make_async_copy(tok, x, load_sem.at[0]),
        pltpu.make_async_copy(down, wd, load_sem.at[1]),
        pltpu.make_async_copy(bfly, w, load_sem.at[2]),
        pltpu.make_async_copy(up, wu, load_sem.at[3]),
    ]
    for load in loads:
        load.start()

    barrier = pltpu.get_barrier_semaphore()
    peers = [(lax.rem(y + d, NY), z) for d in (1, 2, 4, 6, 7)] + [(y, lax.rem(z + d, NZ)) for d in range(1, NZ)]
    for yy, zz in peers:
        pl.semaphore_signal(barrier, inc=1, device_id=at(yy, zz), device_id_type=pl.DeviceIdType.MESH)
    pl.semaphore_wait(barrier, len(peers))

    def chunk(k):
        return pl.ds(k * step, step)

    def own(slot, k, yy, zz):
        return remote(tok.at[chunk(k)], got.at[slot, chunk(k)], send_own.at[slot, k], got_sem.at[slot, k], yy, zz)

    def passed(src, slot, k, yy):
        return remote(got.at[src, chunk(k)], got.at[slot, chunk(k)], pass_sem.at[k], got_sem.at[slot, k], yy, z)

    def send_y(k):
        own(1, k, y2, z).start()
        own(0, k, y1, z).start()

    def send_z(k):
        own(3, k, y, z1).start()
        own(4, k, y, z2).start()

    def wait_got(slot, k):
        own(slot, k, y1, z).wait_recv()

    def share(j, h):
        return pl.ds(pl.multiple_of(j * quarter + h * part_rows, part_rows), part_rows)

    def toward_high(j, h):
        return remote(box.at[share(j, h)], from_low.at[share(j, h)], down_send.at[h, j], low_sem.at[h, j], y, z + 1)

    def toward_low(j, h):
        return remote(box.at[share(j, h)], from_high.at[share(j, h)], down_send.at[h, j], high_sem.at[h, j], y, z - 1)

    def down_step(s, h):
        @pl.when(z <= s)
        def _():
            j = NZ - 1 - s + z

            @pl.when(z > 0)
            def _():
                toward_high(j, h).wait_recv()
                box[share(j, h), :] = (part[share(j, h), :] + from_low[share(j, h), :].astype(F32)).astype(BF16)

            @pl.when(z == 0)
            def _():
                box[share(j, h), :] = part[share(j, h), :].astype(BF16)
            toward_high(j, h).start()

        @pl.when(z >= NZ - 1 - s)
        def _():
            j = s - (NZ - 1) + z

            @pl.when(z < NZ - 1)
            def _():
                toward_low(j, h).wait_recv()
                box[share(j, h), :] = (part[share(j, h), :] + from_high[share(j, h), :].astype(F32)).astype(BF16)

            @pl.when(z == NZ - 1)
            def _():
                box[share(j, h), :] = part[share(j, h), :].astype(BF16)
            toward_low(j, h).start()

    def place(yy):
        return (yy % 2) * half + (yy // 2) * piece

    def piece_at(yy):
        return pl.ds(pl.multiple_of(place(yy), piece), piece)

    def half_at(odd):
        return pl.ds(pl.multiple_of(odd * half, half), half)

    def halve_copy(h):
        return remote(shares.at[h, half_at(1 - b0)], pair_in.at[h], halve_send.at[h], halve_recv.at[h], mate, z)

    def halve(h):
        mine[h] = part[share(z, h), :]

        @pl.when(z > 0)
        def _():
            toward_high(z, h).wait_recv()
            mine[h] += from_low[share(z, h), :].astype(F32)

        @pl.when(z < NZ - 1)
        def _():
            toward_low(z, h).wait_recv()
            mine[h] += from_high[share(z, h), :].astype(F32)
        shares[h, half_at(1 - b0), :] = mine[h, half_at(1 - b0), :].astype(BF16)
        halve_copy(h).start()

    def spread_copy(d, h):
        yy = lax.rem(y + d, NY)
        return remote(shares.at[h, piece_at(yy)], share_in.at[h, d // 2 - 1], spread_send.at[h, d // 2 - 1],
                      spread_recv.at[h, d // 2 - 1], yy, z)

    def spread(h):
        halve_copy(h).wait_recv()
        mine[h, half_at(b0), :] += pair_in[h].astype(F32)
        shares[h, half_at(b0), :] = mine[h, half_at(b0), :].astype(BF16)
        for d in (4, 2, 6):
            spread_copy(d, h).start()

    def mid_rows(start, count, h):
        return pl.ds(pl.multiple_of(z * quarter + h * part_rows + start, piece), count)

    def gather_copy(d, h):
        rows_y = mid_rows(place(y), piece, h)
        return remote(mid.at[rows_y], mid.at[rows_y], gather_send.at[h, d // 2 - 1], gather_recv.at[h, d // 2 - 1],
                      lax.rem(y + d, NY), z)

    def gather(h):
        total = mine[h, piece_at(y), :]
        for d in (2, 4, 6):
            spread_copy(d, h).wait_recv()
            total += share_in[h, d // 2 - 1].astype(F32)
        mid[mid_rows(place(y), piece, h), :] = total.astype(BF16)
        for d in (4, 2, 6):
            gather_copy(d, h).start()

    def join_copy(h):
        rows_half = mid_rows(b0 * half, half, h)
        return remote(mid.at[rows_half], mid.at[rows_half], join_send.at[h], join_recv.at[h], mate, z)

    def join(h):
        for d in (2, 4, 6):
            gather_copy(d, h).wait_recv()
        join_copy(h).start()

    def up_right(j, s, h):
        return remote(mid.at[share(j, h)], mid.at[share(j, h)], up_send_r.at[h, s], up_recv.at[h, j], y, z + 1)

    def up_left(j, s, h):
        return remote(mid.at[share(j, h)], mid.at[share(j, h)], up_send_l.at[h, s], up_recv.at[h, j], y, z - 1)

    def up_step(s, h):
        if s == 0:
            join_copy(h).wait_recv()
        low, high = z - s, z + s

        @pl.when(low >= 0)
        def _():
            if s:
                up_right(low, 0, h).wait_recv()
            if s < NZ - 1:
                @pl.when(z < NZ - 1)
                def _():
                    up_right(low, s, h).start()

        @pl.when(high < NZ)
        def _():
            if s:
                up_left(high, 0, h).wait_recv()
            if s < NZ - 1:
                @pl.when(z > 0)
                def _():
                    up_left(high, s, h).start()

    def pass_a(k):
        wait_got(0, k)

    def pass_b(k):
        wait_got(1, k)
        passed(1, 2, k, y6).start()

    def first_half(k):
        acc[chunk(k), :] = dot(x[chunk(k), :], w[0]) + dot(got[0, chunk(k), :], w[3]) + dot(got[1, chunk(k), :], w[4])

    def project(_):
        loads[0].wait()
        loads[1].wait()

        @pl.loop(0, NZ)
        def _(j):
            rows_j = pl.ds(pl.multiple_of(j * quarter, quarter), quarter)
            part[rows_j, :] = dot(x[rows_j, :], wd[...])

    def weights(_):
        loads[2].wait()
        loads[3].wait()

    outs = []

    def finish(k):
        wait_got(3, k)
        wait_got(4, k)
        wait_got(2, k)
        rows_k = chunk(k)
        dense = (acc[rows_k, :] + dot(got[3, rows_k, :], w[1]) + dot(got[4, rows_k, :], w[2])
                 + dot(got[2, rows_k, :], w[5]) + dot(mid[rows_k, :], wu[...]))
        o[rows_k, :] = (0.5 * dense * (1.0 + lax.erf(dense * 0.7071067811865476))).astype(BF16)
        store = pltpu.make_async_copy(o.at[rows_k], out.at[rows_k], out_sem.at[k])
        store.start()
        outs.append(store)

    steps = {
        "y": send_y, "z": send_z, "a": pass_a, "b": pass_b, "p": first_half, "f": finish,
        "m": project, "w": weights, "h": halve, "s": spread, "g": gather, "j": join,
        "d": lambda i: down_step(i // GROUPS, i % GROUPS), "u": lambda i: up_step(i // GROUPS, i % GROUPS),
    }
    for name, number in plan():
        steps[name](number)

    for k in range(CHUNKS):
        own(0, k, y1, z).wait_send()
        own(3, k, y, z1).wait_send()
        own(4, k, y, z2).wait_send()
        passed(1, 2, k, y6).wait_send()
        own(1, k, y2, z).wait_send()
    for h in range(GROUPS):
        halve_copy(h).wait_send()
        join_copy(h).wait_send()
        for d in (2, 4, 6):
            spread_copy(d, h).wait_send()
            gather_copy(d, h).wait_send()
        for j in range(NZ):
            @pl.when(z != j)
            def _():
                toward_high(j, h).wait_send()
        for s in range(NZ - 1):
            @pl.when((z - s >= 0) & (z < NZ - 1))
            def _():
                up_right(z, s, h).wait_send()

            @pl.when((z + s < NZ) & (z > 0))
            def _():
                up_left(z, s, h).wait_send()
    for store in outs:
        store.wait()


def shards(tokens, butterfly, rank_down, rank_up):
    rows, width = tokens.shape
    rank = rank_down.shape[1]
    quarter = rows // NZ
    part_rows = quarter // GROUPS
    piece = part_rows // NY
    dma = pltpu.SemaphoreType.DMA
    vmem = pltpu.VMEM
    anywhere = pl.BlockSpec(memory_space=pl.ANY)
    return pl.pallas_call(
        kernel,
        out_shape=jax.ShapeDtypeStruct((rows, width), BF16),
        in_specs=[anywhere] * 4,
        out_specs=anywhere,
        scratch_shapes=[
            vmem((rows, width), BF16),
            vmem(butterfly.shape, BF16),
            vmem(rank_down.shape, BF16),
            vmem(rank_up.shape, BF16),
            vmem((5, rows, width), BF16),
            vmem((rows, width), F32),
            vmem((rows, rank), F32),
            vmem((rows, rank), BF16),
            vmem((rows, rank), BF16),
            vmem((rows, rank), BF16),
            vmem((GROUPS, part_rows, rank), F32),
            vmem((GROUPS, part_rows, rank), BF16),
            vmem((GROUPS, part_rows // 2, rank), BF16),
            vmem((GROUPS, 3, piece, rank), BF16),
            vmem((rows, rank), BF16),
            vmem((rows, width), BF16),
            dma((4,)), dma((5, CHUNKS)), dma((5, CHUNKS)), dma((CHUNKS,)),
            dma((GROUPS, NZ)), dma((GROUPS, NZ)), dma((GROUPS, NZ)), dma((GROUPS,)), dma((GROUPS,)), dma((GROUPS, 3)), dma((GROUPS, 3)),
            dma((GROUPS, 3)), dma((GROUPS, 3)), dma((GROUPS,)), dma((GROUPS,)), dma((GROUPS, NZ - 1)), dma((GROUPS, NZ - 1)), dma((GROUPS, NZ)),
            dma((CHUNKS,)),
        ],
        compiler_params=pltpu.CompilerParams(
            collective_id=0, has_side_effects=True, vmem_limit_bytes=63 * 2**20),
        cost_estimate=pl.CostEstimate(
            flops=2 * rows * width * width * 8, bytes_accessed=6 * 2**20, transcendentals=rows * width),
    )(tokens, butterfly, rank_down, rank_up)


def solution(mesh):
    return jax.shard_map(
        shards,
        mesh=mesh,
        in_specs=(P("tok", "feat"), P(None, None, "feat"), P("feat", None), P(None, "feat")),
        out_specs=P("tok", "feat"),
        check_vma=False,
    )
```

```python
import functools

import jax
import jax.numpy as jnp
from jax import lax
from jax.experimental import pallas as pl
from jax.experimental.pallas import tpu as pltpu
from jax.sharding import PartitionSpec as P

CHUNKS = 8
GROUPS = 2


def plan():
    order = [('y', 0), ('m', 0), ('d', 0), ('d', 1), ('w', 0), ('y', 1), ('a', 0), ('d', 2), ('d', 3), ('z', 0), ('b', 0), ('y', 2), ('a', 1), ('d', 4), ('d', 5), ('z', 1), ('z', 2), ('p', 0), ('b', 1), ('y', 3), ('a', 2), ('h', 0), ('h', 1), ('z', 3), ('z', 4), ('p', 1), ('b', 2), ('y', 4), ('a', 3), ('s', 0), ('s', 1), ('g', 0), ('g', 1), ('z', 5), ('z', 6), ('p', 2), ('b', 3), ('y', 5), ('a', 4), ('j', 0), ('j', 1), ('z', 7), ('p', 3), ('b', 4), ('y', 6), ('a', 5), ('u', 0), ('u', 1), ('p', 4), ('y', 7), ('a', 6), ('b', 5), ('u', 2), ('u', 3), ('p', 5), ('a', 7), ('b', 6), ('u', 4), ('u', 5), ('p', 6), ('b', 7), ('u', 6), ('u', 7), ('p', 7), ('f', 0), ('f', 1), ('f', 2), ('f', 3), ('f', 4), ('f', 5), ('f', 6), ('f', 7)]
    return order


NY, NZ = 8, 4
F32, BF16 = jnp.float32, jnp.bfloat16


def dot(a, b):
    return jnp.dot(a, b, preferred_element_type=F32)


def kernel(tok, bfly, down, up, out,
           x, w, wd, wu, got, acc, part, box, from_low, from_high, mine, shares, pair_in, share_in, mid, o,
           load_sem, send_own, got_sem, pass_sem, down_send, low_sem, high_sem, halve_send, halve_recv, spread_send, spread_recv,
           gather_send, gather_recv, join_send, join_recv, up_send_r, up_send_l, up_recv, out_sem):
    rows = tok.shape[0]
    step = rows // CHUNKS
    quarter = rows // NZ
    part_rows = quarter // GROUPS
    half = part_rows // 2
    piece = part_rows // NY
    me = lax.axis_index("feat")
    y, z = me // NZ, me % NZ
    b0, b1, b2 = y % 2, (y // 2) % 2, y // 4
    y1 = y + 1 - 2 * b0
    y2 = y + 2 - 4 * b1
    y6 = y2 + 4 - 8 * b2
    mate = lax.rem(y + NY - 1 + 2 * b0, NY)
    z1 = z + 1 - 2 * (z % 2)
    z2 = z + 2 - 4 * (z // 2)

    def at(yy, zz):
        return {"feat": yy * NZ + zz}

    def remote(src, dst, ssem, rsem, yy, zz):
        return pltpu.make_async_remote_copy(
            src_ref=src, dst_ref=dst, send_sem=ssem, recv_sem=rsem,
            device_id=at(yy, zz), device_id_type=pl.DeviceIdType.MESH)

    loads = [
        pltpu.make_async_copy(tok, x, load_sem.at[0]),
        pltpu.make_async_copy(down, wd, load_sem.at[1]),
        pltpu.make_async_copy(bfly, w, load_sem.at[2]),
        pltpu.make_async_copy(up, wu, load_sem.at[3]),
    ]
    for load in loads:
        load.start()

    barrier = pltpu.get_barrier_semaphore()
    peers = [(lax.rem(y + d, NY), z) for d in (1, 2, 4, 6, 7)] + [(y, lax.rem(z + d, NZ)) for d in range(1, NZ)]
    for yy, zz in peers:
        pl.semaphore_signal(barrier, inc=1, device_id=at(yy, zz), device_id_type=pl.DeviceIdType.MESH)
    pl.semaphore_wait(barrier, len(peers))

    def chunk(k):
        return pl.ds(k * step, step)

    def own(slot, k, yy, zz):
        return remote(x.at[chunk(k)], got.at[slot, chunk(k)], send_own.at[slot, k], got_sem.at[slot, k], yy, zz)

    def passed(src, slot, k, yy):
        return remote(got.at[src, chunk(k)], got.at[slot, chunk(k)], pass_sem.at[k], got_sem.at[slot, k], yy, z)

    def send_y(k):
        own(1, k, y2, z).start()
        own(0, k, y1, z).start()

    def send_z(k):
        own(3, k, y, z1).start()
        own(4, k, y, z2).start()

    def wait_got(slot, k):
        own(slot, k, y1, z).wait_recv()

    def share(j, h):
        return pl.ds(pl.multiple_of(j * quarter + h * part_rows, part_rows), part_rows)

    def toward_high(j, h):
        return remote(box.at[share(j, h)], from_low.at[share(j, h)], down_send.at[h, j], low_sem.at[h, j], y, z + 1)

    def toward_low(j, h):
        return remote(box.at[share(j, h)], from_high.at[share(j, h)], down_send.at[h, j], high_sem.at[h, j], y, z - 1)

    def down_step(s, h):
        @pl.when(z <= s)
        def _():
            j = NZ - 1 - s + z

            @pl.when(z > 0)
            def _():
                toward_high(j, h).wait_recv()
                box[share(j, h), :] = (part[share(j, h), :] + from_low[share(j, h), :].astype(F32)).astype(BF16)

            @pl.when(z == 0)
            def _():
                box[share(j, h), :] = part[share(j, h), :].astype(BF16)
            toward_high(j, h).start()

        @pl.when(z >= NZ - 1 - s)
        def _():
            j = s - (NZ - 1) + z

            @pl.when(z < NZ - 1)
            def _():
                toward_low(j, h).wait_recv()
                box[share(j, h), :] = (part[share(j, h), :] + from_high[share(j, h), :].astype(F32)).astype(BF16)

            @pl.when(z == NZ - 1)
            def _():
                box[share(j, h), :] = part[share(j, h), :].astype(BF16)
            toward_low(j, h).start()

    def place(yy):
        return (yy % 2) * half + (yy // 2) * piece

    def piece_at(yy):
        return pl.ds(pl.multiple_of(place(yy), piece), piece)

    def half_at(odd):
        return pl.ds(pl.multiple_of(odd * half, half), half)

    def halve_copy(h):
        return remote(shares.at[h, half_at(1 - b0)], pair_in.at[h], halve_send.at[h], halve_recv.at[h], mate, z)

    def halve(h):
        mine[h] = part[share(z, h), :]

        @pl.when(z > 0)
        def _():
            toward_high(z, h).wait_recv()
            mine[h] += from_low[share(z, h), :].astype(F32)

        @pl.when(z < NZ - 1)
        def _():
            toward_low(z, h).wait_recv()
            mine[h] += from_high[share(z, h), :].astype(F32)
        shares[h, half_at(1 - b0), :] = mine[h, half_at(1 - b0), :].astype(BF16)
        halve_copy(h).start()

    def spread_copy(d, h):
        yy = lax.rem(y + d, NY)
        return remote(shares.at[h, piece_at(yy)], share_in.at[h, d // 2 - 1], spread_send.at[h, d // 2 - 1],
                      spread_recv.at[h, d // 2 - 1], yy, z)

    def spread(h):
        halve_copy(h).wait_recv()
        mine[h, half_at(b0), :] += pair_in[h].astype(F32)
        shares[h, half_at(b0), :] = mine[h, half_at(b0), :].astype(BF16)
        for d in (4, 2, 6):
            spread_copy(d, h).start()

    def mid_rows(start, count, h):
        return pl.ds(pl.multiple_of(z * quarter + h * part_rows + start, piece), count)

    def gather_copy(d, h):
        rows_y = mid_rows(place(y), piece, h)
        return remote(mid.at[rows_y], mid.at[rows_y], gather_send.at[h, d // 2 - 1], gather_recv.at[h, d // 2 - 1],
                      lax.rem(y + d, NY), z)

    def gather(h):
        total = mine[h, piece_at(y), :]
        for d in (2, 4, 6):
            spread_copy(d, h).wait_recv()
            total += share_in[h, d // 2 - 1].astype(F32)
        mid[mid_rows(place(y), piece, h), :] = total.astype(BF16)
        for d in (4, 2, 6):
            gather_copy(d, h).start()

    def join_copy(h):
        rows_half = mid_rows(b0 * half, half, h)
        return remote(mid.at[rows_half], mid.at[rows_half], join_send.at[h], join_recv.at[h], mate, z)

    def join(h):
        for d in (2, 4, 6):
            gather_copy(d, h).wait_recv()
        join_copy(h).start()

    def up_right(j, s, h):
        return remote(mid.at[share(j, h)], mid.at[share(j, h)], up_send_r.at[h, s], up_recv.at[h, j], y, z + 1)

    def up_left(j, s, h):
        return remote(mid.at[share(j, h)], mid.at[share(j, h)], up_send_l.at[h, s], up_recv.at[h, j], y, z - 1)

    def up_step(s, h):
        if s == 0:
            join_copy(h).wait_recv()
        low, high = z - s, z + s

        @pl.when(low >= 0)
        def _():
            if s:
                up_right(low, 0, h).wait_recv()
            if s < NZ - 1:
                @pl.when(z < NZ - 1)
                def _():
                    up_right(low, s, h).start()

        @pl.when(high < NZ)
        def _():
            if s:
                up_left(high, 0, h).wait_recv()
            if s < NZ - 1:
                @pl.when(z > 0)
                def _():
                    up_left(high, s, h).start()

    def pass_a(k):
        wait_got(0, k)

    def pass_b(k):
        wait_got(1, k)
        passed(1, 2, k, y6).start()

    def first_half(k):
        acc[chunk(k), :] = dot(x[chunk(k), :], w[0]) + dot(got[0, chunk(k), :], w[3]) + dot(got[1, chunk(k), :], w[4])

    def project(_):
        loads[1].wait()

        @pl.loop(0, NZ)
        def _(j):
            rows_j = pl.ds(pl.multiple_of(j * quarter, quarter), quarter)
            part[rows_j, :] = dot(x[rows_j, :], wd[...])

    def weights(_):
        loads[2].wait()
        loads[3].wait()

    outs = []

    def finish(k):
        wait_got(3, k)
        wait_got(4, k)
        wait_got(2, k)
        rows_k = chunk(k)
        dense = (acc[rows_k, :] + dot(got[3, rows_k, :], w[1]) + dot(got[4, rows_k, :], w[2])
                 + dot(got[2, rows_k, :], w[5]) + dot(mid[rows_k, :], wu[...]))
        o[rows_k, :] = (0.5 * dense * (1.0 + lax.erf(dense * 0.7071067811865476))).astype(BF16)
        store = pltpu.make_async_copy(o.at[rows_k], out.at[rows_k], out_sem.at[k])
        store.start()
        outs.append(store)

    steps = {
        "y": send_y, "z": send_z, "a": pass_a, "b": pass_b, "p": first_half, "f": finish,
        "m": project, "w": weights, "h": halve, "s": spread, "g": gather, "j": join,
        "d": lambda i: down_step(i // GROUPS, i % GROUPS), "u": lambda i: up_step(i // GROUPS, i % GROUPS),
    }
    loads[0].wait()
    for name, number in plan():
        steps[name](number)

    for k in range(CHUNKS):
        own(0, k, y1, z).wait_send()
        own(3, k, y, z1).wait_send()
        own(4, k, y, z2).wait_send()
        passed(1, 2, k, y6).wait_send()
        own(1, k, y2, z).wait_send()
    for h in range(GROUPS):
        halve_copy(h).wait_send()
        join_copy(h).wait_send()
        for d in (2, 4, 6):
            spread_copy(d, h).wait_send()
            gather_copy(d, h).wait_send()
        for j in range(NZ):
            @pl.when(z != j)
            def _():
                toward_high(j, h).wait_send()
        for s in range(NZ - 1):
            @pl.when((z - s >= 0) & (z < NZ - 1))
            def _():
                up_right(z, s, h).wait_send()

            @pl.when((z + s < NZ) & (z > 0))
            def _():
                up_left(z, s, h).wait_send()
    for store in outs:
        store.wait()


def shards(tokens, butterfly, rank_down, rank_up):
    rows, width = tokens.shape
    rank = rank_down.shape[1]
    quarter = rows // NZ
    part_rows = quarter // GROUPS
    piece = part_rows // NY
    dma = pltpu.SemaphoreType.DMA
    vmem = pltpu.VMEM
    anywhere = pl.BlockSpec(memory_space=pl.ANY)
    return pl.pallas_call(
        kernel,
        out_shape=jax.ShapeDtypeStruct((rows, width), BF16),
        in_specs=[anywhere] * 4,
        out_specs=anywhere,
        scratch_shapes=[
            vmem((rows, width), BF16),
            vmem(butterfly.shape, BF16),
            vmem(rank_down.shape, BF16),
            vmem(rank_up.shape, BF16),
            vmem((5, rows, width), BF16),
            vmem((rows, width), F32),
            vmem((rows, rank), F32),
            vmem((rows, rank), BF16),
            vmem((rows, rank), BF16),
            vmem((rows, rank), BF16),
            vmem((GROUPS, part_rows, rank), F32),
            vmem((GROUPS, part_rows, rank), BF16),
            vmem((GROUPS, part_rows // 2, rank), BF16),
            vmem((GROUPS, 3, piece, rank), BF16),
            vmem((rows, rank), BF16),
            vmem((rows, width), BF16),
            dma((4,)), dma((5, CHUNKS)), dma((5, CHUNKS)), dma((CHUNKS,)),
            dma((GROUPS, NZ)), dma((GROUPS, NZ)), dma((GROUPS, NZ)), dma((GROUPS,)), dma((GROUPS,)), dma((GROUPS, 3)), dma((GROUPS, 3)),
            dma((GROUPS, 3)), dma((GROUPS, 3)), dma((GROUPS,)), dma((GROUPS,)), dma((GROUPS, NZ - 1)), dma((GROUPS, NZ - 1)), dma((GROUPS, NZ)),
            dma((CHUNKS,)),
        ],
        compiler_params=pltpu.CompilerParams(
            collective_id=0, has_side_effects=True, vmem_limit_bytes=63 * 2**20),
        cost_estimate=pl.CostEstimate(
            flops=2 * rows * width * width * 8, bytes_accessed=6 * 2**20, transcendentals=rows * width),
    )(tokens, butterfly, rank_down, rank_up)


def solution(mesh):
    return jax.shard_map(
        shards,
        mesh=mesh,
        in_specs=(P("tok", "feat"), P(None, None, "feat"), P("feat", None), P(None, "feat")),
        out_specs=P("tok", "feat"),
        check_vma=False,
    )
```

```python
import functools

import jax
import jax.numpy as jnp
from jax import lax
from jax.experimental import pallas as pl
from jax.experimental.pallas import tpu as pltpu
from jax.sharding import PartitionSpec as P

CHUNKS = 8
GROUPS = 2


def plan():
    order = [('y', 0), ('m', 0), ('d', 0), ('d', 1), ('w', 0), ('y', 1), ('a', 0), ('d', 2), ('d', 3), ('z', 0), ('b', 0), ('y', 2), ('a', 1), ('d', 4), ('d', 5), ('z', 1), ('z', 2), ('p', 0), ('b', 1), ('y', 3), ('a', 2), ('h', 0), ('h', 1), ('z', 3), ('z', 4), ('p', 1), ('b', 2), ('y', 4), ('a', 3), ('s', 0), ('s', 1), ('g', 0), ('g', 1), ('z', 5), ('z', 6), ('p', 2), ('b', 3), ('y', 5), ('a', 4), ('j', 0), ('j', 1), ('z', 7), ('p', 3), ('b', 4), ('y', 6), ('a', 5), ('u', 0), ('u', 1), ('p', 4), ('y', 7), ('a', 6), ('b', 5), ('u', 2), ('u', 3), ('p', 5), ('a', 7), ('b', 6), ('u', 4), ('u', 5), ('p', 6), ('b', 7), ('u', 6), ('u', 7), ('p', 7), ('f', 0), ('f', 1), ('f', 2), ('f', 3), ('f', 4), ('f', 5), ('f', 6), ('f', 7)]
    return order


NY, NZ = 8, 4
F32, BF16 = jnp.float32, jnp.bfloat16


def dot(a, b):
    return jnp.dot(a, b, preferred_element_type=F32)


def kernel(tok, bfly, down, up, out,
           x, w, wd, wu, got, acc, part, box, from_low, from_high, mine, shares, pair_in, share_in, mid, o,
           load_sem, send_own, got_sem, pass_sem, down_send, low_sem, high_sem, halve_send, halve_recv, spread_send, spread_recv,
           gather_send, gather_recv, join_send, join_recv, up_send_r, up_send_l, up_recv, out_sem):
    rows = tok.shape[0]
    step = rows // CHUNKS
    quarter = rows // NZ
    part_rows = quarter // GROUPS
    half = part_rows // 2
    piece = part_rows // NY
    me = lax.axis_index("feat")
    y, z = me // NZ, me % NZ
    b0, b1, b2 = y % 2, (y // 2) % 2, y // 4
    y1 = y + 1 - 2 * b0
    y2 = y + 2 - 4 * b1
    y6 = y2 + 4 - 8 * b2
    mate = lax.rem(y + NY - 1 + 2 * b0, NY)
    z1 = z + 1 - 2 * (z % 2)
    z2 = z + 2 - 4 * (z // 2)

    def at(yy, zz):
        return {"feat": yy * NZ + zz}

    def remote(src, dst, ssem, rsem, yy, zz):
        return pltpu.make_async_remote_copy(
            src_ref=src, dst_ref=dst, send_sem=ssem, recv_sem=rsem,
            device_id=at(yy, zz), device_id_type=pl.DeviceIdType.MESH)

    loads = [
        pltpu.make_async_copy(tok, x, load_sem.at[0]),
        pltpu.make_async_copy(down, wd, load_sem.at[1]),
        pltpu.make_async_copy(bfly, w, load_sem.at[2]),
        pltpu.make_async_copy(up, wu, load_sem.at[3]),
    ]
    for load in loads:
        load.start()

    barrier = pltpu.get_barrier_semaphore()
    peers = [(lax.rem(y + d, NY), z) for d in (1, 2, 4, 6, 7)] + [(y, lax.rem(z + d, NZ)) for d in range(1, NZ)]
    for yy, zz in peers:
        pl.semaphore_signal(barrier, inc=1, device_id=at(yy, zz), device_id_type=pl.DeviceIdType.MESH)
    pl.semaphore_wait(barrier, len(peers))

    def chunk(k):
        return pl.ds(k * step, step)

    def own(slot, k, yy, zz):
        return remote(x.at[chunk(k)], got.at[slot, chunk(k)], send_own.at[slot, k], got_sem.at[slot, k], yy, zz)

    def passed(src, slot, k, yy):
        return remote(got.at[src, chunk(k)], got.at[slot, chunk(k)], pass_sem.at[k], got_sem.at[slot, k], yy, z)

    def send_y(k):
        own(1, k, y2, z).start()
        own(0, k, y1, z).start()

    def send_z(k):
        own(3, k, y, z1).start()
        own(4, k, y, z2).start()

    def wait_got(slot, k):
        own(slot, k, y1, z).wait_recv()

    def share(j, h):
        return pl.ds(pl.multiple_of(j * quarter + h * part_rows, part_rows), part_rows)

    def toward_high(j, h):
        return remote(box.at[share(j, h)], from_low.at[share(j, h)], down_send.at[h, j], low_sem.at[h, j], y, z + 1)

    def toward_low(j, h):
        return remote(box.at[share(j, h)], from_high.at[share(j, h)], down_send.at[h, j], high_sem.at[h, j], y, z - 1)

    def down_step(s, h):
        @pl.when(z <= s)
        def _():
            j = NZ - 1 - s + z

            @pl.when(z > 0)
            def _():
                toward_high(j, h).wait_recv()
                box[share(j, h), :] = (part[share(j, h), :] + from_low[share(j, h), :].astype(F32)).astype(BF16)

            @pl.when(z == 0)
            def _():
                box[share(j, h), :] = part[share(j, h), :].astype(BF16)
            toward_high(j, h).start()

        @pl.when(z >= NZ - 1 - s)
        def _():
            j = s - (NZ - 1) + z

            @pl.when(z < NZ - 1)
            def _():
                toward_low(j, h).wait_recv()
                box[share(j, h), :] = (part[share(j, h), :] + from_high[share(j, h), :].astype(F32)).astype(BF16)

            @pl.when(z == NZ - 1)
            def _():
                box[share(j, h), :] = part[share(j, h), :].astype(BF16)
            toward_low(j, h).start()

    def place(yy):
        return (yy % 2) * half + (yy // 2) * piece

    def piece_at(yy):
        return pl.ds(pl.multiple_of(place(yy), piece), piece)

    def half_at(odd):
        return pl.ds(pl.multiple_of(odd * half, half), half)

    def halve_copy(h):
        return remote(shares.at[h, half_at(1 - b0)], pair_in.at[h], halve_send.at[h], halve_recv.at[h], mate, z)

    def halve(h):
        mine[h] = part[share(z, h), :]

        @pl.when(z > 0)
        def _():
            toward_high(z, h).wait_recv()
            mine[h] += from_low[share(z, h), :].astype(F32)

        @pl.when(z < NZ - 1)
        def _():
            toward_low(z, h).wait_recv()
            mine[h] += from_high[share(z, h), :].astype(F32)
        shares[h, half_at(1 - b0), :] = mine[h, half_at(1 - b0), :].astype(BF16)
        halve_copy(h).start()

    def spread_copy(d, h):
        yy = lax.rem(y + d, NY)
        return remote(shares.at[h, piece_at(yy)], share_in.at[h, d // 2 - 1], spread_send.at[h, d // 2 - 1],
                      spread_recv.at[h, d // 2 - 1], yy, z)

    def spread(h):
        halve_copy(h).wait_recv()
        mine[h, half_at(b0), :] += pair_in[h].astype(F32)
        shares[h, half_at(b0), :] = mine[h, half_at(b0), :].astype(BF16)
        for d in (4, 2, 6):
            spread_copy(d, h).start()

    def mid_rows(start, count, h):
        return pl.ds(pl.multiple_of(z * quarter + h * part_rows + start, piece), count)

    def gather_copy(d, h):
        rows_y = mid_rows(place(y), piece, h)
        return remote(mid.at[rows_y], mid.at[rows_y], gather_send.at[h, d // 2 - 1], gather_recv.at[h, d // 2 - 1],
                      lax.rem(y + d, NY), z)

    def gather(h):
        total = mine[h, piece_at(y), :]
        for d in (2, 4, 6):
            spread_copy(d, h).wait_recv()
            total += share_in[h, d // 2 - 1].astype(F32)
        mid[mid_rows(place(y), piece, h), :] = total.astype(BF16)
        for d in (4, 2, 6):
            gather_copy(d, h).start()

    def join_copy(h):
        rows_half = mid_rows(b0 * half, half, h)
        return remote(mid.at[rows_half], mid.at[rows_half], join_send.at[h], join_recv.at[h], mate, z)

    def join(h):
        for d in (2, 4, 6):
            gather_copy(d, h).wait_recv()
        join_copy(h).start()

    def up_right(j, s, h):
        return remote(mid.at[share(j, h)], mid.at[share(j, h)], up_send_r.at[h, s], up_recv.at[h, j], y, z + 1)

    def up_left(j, s, h):
        return remote(mid.at[share(j, h)], mid.at[share(j, h)], up_send_l.at[h, s], up_recv.at[h, j], y, z - 1)

    def up_step(s, h):
        if s == 0:
            join_copy(h).wait_recv()
        low, high = z - s, z + s

        @pl.when(low >= 0)
        def _():
            if s:
                up_right(low, 0, h).wait_recv()
            if s < NZ - 1:
                @pl.when(z < NZ - 1)
                def _():
                    up_right(low, s, h).start()

        @pl.when(high < NZ)
        def _():
            if s:
                up_left(high, 0, h).wait_recv()
            if s < NZ - 1:
                @pl.when(z > 0)
                def _():
                    up_left(high, s, h).start()

    def pass_a(k):
        wait_got(0, k)

    def pass_b(k):
        wait_got(1, k)
        passed(1, 2, k, y6).start()

    def first_half(k):
        acc[chunk(k), :] = dot(x[chunk(k), :], w[0]) + dot(got[0, chunk(k), :], w[3]) + dot(got[1, chunk(k), :], w[4])

    def project(_):
        loads[1].wait()

        @pl.loop(0, NZ)
        def _(j):
            rows_j = pl.ds(pl.multiple_of(j * quarter, quarter), quarter)
            part[rows_j, :] = dot(x[rows_j, :], wd[...])

    def weights(_):
        loads[2].wait()
        loads[3].wait()

    outs = []

    def finish(k):
        wait_got(3, k)
        wait_got(4, k)
        wait_got(2, k)
        rows_k = chunk(k)
        dense = (acc[rows_k, :] + dot(got[3, rows_k, :], w[1]) + dot(got[4, rows_k, :], w[2])
                 + dot(got[2, rows_k, :], w[5]) + dot(mid[rows_k, :], wu[...]))
        o[rows_k, :] = (0.5 * dense * (1.0 + lax.erf(dense * 0.7071067811865476))).astype(BF16)
        store = pltpu.make_async_copy(o.at[rows_k], out.at[rows_k], out_sem.at[k])
        store.start()
        outs.append(store)

    steps = {
        "y": send_y, "z": send_z, "a": pass_a, "b": pass_b, "p": first_half, "f": finish,
        "m": project, "w": weights, "h": halve, "s": spread, "g": gather, "j": join,
        "d": lambda i: down_step(i // GROUPS, i % GROUPS), "u": lambda i: up_step(i // GROUPS, i % GROUPS),
    }
    loads[0].wait()
    for name, number in plan():
        steps[name](number)

    for k in range(CHUNKS):
        own(0, k, y1, z).wait_send()
        own(3, k, y, z1).wait_send()
        own(4, k, y, z2).wait_send()
        passed(1, 2, k, y6).wait_send()
        own(1, k, y2, z).wait_send()
    for h in range(GROUPS):
        halve_copy(h).wait_send()
        join_copy(h).wait_send()
        for d in (2, 4, 6):
            spread_copy(d, h).wait_send()
            gather_copy(d, h).wait_send()
        for j in range(NZ):
            @pl.when(z != j)
            def _():
                toward_high(j, h).wait_send()
        for s in range(NZ - 1):
            @pl.when((z - s >= 0) & (z < NZ - 1))
            def _():
                up_right(z, s, h).wait_send()

            @pl.when((z + s < NZ) & (z > 0))
            def _():
                up_left(z, s, h).wait_send()
    for store in outs:
        store.wait()


def shards(tokens, butterfly, rank_down, rank_up):
    rows, width = tokens.shape
    rank = rank_down.shape[1]
    quarter = rows // NZ
    part_rows = quarter // GROUPS
    piece = part_rows // NY
    dma = pltpu.SemaphoreType.DMA
    vmem = pltpu.VMEM
    anywhere = pl.BlockSpec(memory_space=pl.ANY)
    return pl.pallas_call(
        kernel,
        out_shape=jax.ShapeDtypeStruct((rows, width), BF16),
        in_specs=[anywhere] * 4,
        out_specs=anywhere,
        scratch_shapes=[
            vmem((rows, width), BF16),
            vmem(butterfly.shape, BF16),
            vmem(rank_down.shape, BF16),
            vmem(rank_up.shape, BF16),
            vmem((5, rows, width), BF16),
            vmem((rows, width), F32),
            vmem((rows, rank), F32),
            vmem((rows, rank), BF16),
            vmem((rows, rank), BF16),
            vmem((rows, rank), BF16),
            vmem((GROUPS, part_rows, rank), F32),
            vmem((GROUPS, part_rows, rank), BF16),
            vmem((GROUPS, part_rows // 2, rank), BF16),
            vmem((GROUPS, 3, piece, rank), BF16),
            vmem((rows, rank), BF16),
            vmem((rows, width), BF16),
            dma((4,)), dma((5, CHUNKS)), dma((5, CHUNKS)), dma((CHUNKS,)),
            dma((GROUPS, NZ)), dma((GROUPS, NZ)), dma((GROUPS, NZ)), dma((GROUPS,)), dma((GROUPS,)), dma((GROUPS, 3)), dma((GROUPS, 3)),
            dma((GROUPS, 3)), dma((GROUPS, 3)), dma((GROUPS,)), dma((GROUPS,)), dma((GROUPS, NZ - 1)), dma((GROUPS, NZ - 1)), dma((GROUPS, NZ)),
            dma((CHUNKS,)),
        ],
        compiler_params=pltpu.CompilerParams(
            collective_id=0, has_side_effects=True, vmem_limit_bytes=51 * 2**20),
        cost_estimate=pl.CostEstimate(
            flops=2 * rows * width * width * 8, bytes_accessed=6 * 2**20, transcendentals=rows * width),
    )(tokens, butterfly, rank_down, rank_up)


def solution(mesh):
    return jax.shard_map(
        shards,
        mesh=mesh,
        in_specs=(P("tok", "feat"), P(None, None, "feat"), P("feat", None), P(None, "feat")),
        out_specs=P("tok", "feat"),
        check_vma=False,
    )
```
